128 devices in a mesh: gx: 4 (over y_lo, core), gy: 4 (over z), gz: 8 (over x, y_hi).
Axes of the slice: x: 4, y: 4 (y_hi: 2, y_lo: 2; y = y_hi * 2 + y_lo), z: 4, core: 2. Of those that a mesh axis runs over, the one named last changes fastest.
Arguments:
- wave_bands: bfloat16 [96, 96, 256, 256], P('gx', 'gy', 'gz'), may hold values from -6 to 6
- potential: float32 [32, 32, 128], P('gx', 'gy', 'gz'), may hold values from -1 to 1
- occupation: float32 [4, 4, 8, 256], P('gx', 'gy', 'gz'), may hold values from 0.001 to 0.008
- support: float32 [96, 96, 256], P('gx', 'gy', 'gz'), may hold values from 0.25 to 1
- z_cuts: int32 [9], replicated, may hold values from 0 to 128, as said below
- atom_state: float32 [4, 16384], P(None, ('gx', 'gy', 'gz')), may hold values from -6 to 6
- atom_cell: int32 [16384], P(('gx', 'gy', 'gz')), may hold values from 0 to 127, as said below
Outputs:
- density: float32 [32, 32, 128], P('gx', 'gy', 'gz')
- new_bands: bfloat16 [96, 96, 320, 256], P('gx', 'gy', 'gz')
- new_atoms: float32 [4, 32768], P(None, ('gx', 'gy', 'gz'))
- new_cells: int32 [32768], P(('gx', 'gy', 'gz'))
The draws below stay inside these ranges and needn't reach their ends.
Inputs may be any that keep to these rules, and one draw needn't show every extreme that they name: `z_cuts`: entry k is k * 16 plus an offset from 0 to 8; the first and the last offsets are 0; where there are two or more interior cuts, some offset is exactly 8. `atom_cell`: the atoms of a domain with z index c lie in cells c * 16 to c * 16 + 15.
All inputs are finite; a program needn't handle non-finite values.
Results may differ from the reference program's by a relative error of at most 0.012.
Values may be sent and summed in bfloat16 or wider, within the bound.
No kernel may reach another device: no remote copies, remote signals or barrier semaphores. Data moves between devices by JAX's collectives and lax.ppermute only.
A program may use at most 192 MiB of HBM per device.

```python
import math
import jax
import jax.numpy as jnp
from jax import lax

NB = 256
B = 8
SWEEPS = 2
COMP = 4
CX = 8
CY = 8
CZ = 16
ATOMS_DEV = 128
DX = 24
DY = 24
DZ = 32
DRIFT = 8
DZCAP = 40
NX = 32
NY = 32
NZ = 128
CUTS = 9
NATOM = 16384
ACAP = 256
N_GX = 4
N_GY = 4
N_GZ = 8
DEVICES = 128


def draw_z_cuts(key, part):
    key = jax.random.fold_in(key, 11)
    offset_key, pick_key = jax.random.split(key)
    positions = jnp.arange(CUTS, dtype=jnp.int32)
    offsets = jax.random.randint(offset_key, (CUTS,), 0, DRIFT + 1, dtype=jnp.int32)
    if N_GZ > 2:
        chosen = jax.random.randint(pick_key, (), 1, N_GZ, dtype=jnp.int32)
        offsets = jnp.where(positions == chosen, DRIFT, offsets)
    offsets = jnp.where(jnp.logical_or(positions == 0, positions == N_GZ), 0, offsets)
    return positions * CZ + offsets


def draw_atom_cell(key, part):
    key = jax.random.fold_in(key, 7)
    slot_ids = jnp.arange(NATOM, dtype=jnp.int32)
    slab_ids = slot_ids // ATOMS_DEV % N_GZ
    return slab_ids * CZ + jax.random.randint(key, (NATOM,), 0, CZ, dtype=jnp.int32)


def shard_levels(key, dims, pieces, smallest, high):
    factor_of, own = 1.0, jax.random.fold_in(key, 6)
    for position, blocks in pieces:
        steps = jnp.exp(jax.random.uniform(jax.random.fold_in(own, position), (blocks,), jnp.float32, smallest / len(pieces), high / len(pieces)))
        factor_of = factor_of * jnp.repeat(steps, dims[position] // blocks).reshape([-1 if axis == position else 1 for axis in range(len(dims))])
    return factor_of


def noise(key, shape, width, limit, cuts=(), held_as=jnp.bfloat16):
    drawn = width * jax.random.normal(key, shape, jnp.float32)
    if cuts:
        drawn = drawn * shard_levels(key, shape, cuts, -0.22, 0.18)
    return jnp.clip(drawn, -limit, limit).astype(held_as)


def setup_inputs(seed: int = 0) -> dict:
    seeds = jax.random.split(jax.random.key(seed), 8)
    wave_bands = noise(seeds[0], (DX * N_GX, DY * N_GY, DZ * N_GZ, NB), 1.0, 6.0, ((0, 4), (1, 4), (2, 8)))
    potential = jnp.clip(jax.random.uniform(seeds[1], (NX, NY, NZ), jnp.float32, -1.0, 1.0) * shard_levels(seeds[1], (NX, NY, NZ), ((0, 4), (1, 4), (2, 8)), -0.4, 0.0), -1.0, 1.0)
    occupation = jnp.clip(jnp.exp(math.log(0.008) - 2.0794415 * jax.random.uniform(seeds[2], (N_GX, N_GY, N_GZ, NB), jnp.float32) ** shard_levels(seeds[2], (N_GX, N_GY, N_GZ, NB), ((0, 4), (1, 4), (2, 8)), -0.2, 0.2)), 0.001, 0.008)
    support = jnp.clip(0.25 + 0.75 * jax.random.uniform(seeds[3], (DX * N_GX, DY * N_GY, DZ * N_GZ), jnp.float32) ** shard_levels(seeds[3], (DX * N_GX, DY * N_GY, DZ * N_GZ), ((0, 4), (1, 4), (2, 8)), -0.2, 0.2), 0.25, 1.0)
    z_cuts = draw_z_cuts(jax.random.fold_in(seeds[7], 71), 0)
    atom_state = noise(seeds[5], (COMP, NATOM), 1.0, 6.0, ((1, 128),), jnp.float32)
    atom_cell = draw_atom_cell(jax.random.fold_in(seeds[7], 71), 0)
    return dict(wave_bands=wave_bands, potential=potential, occupation=occupation, support=support, z_cuts=z_cuts, atom_state=atom_state, atom_cell=atom_cell)


step_size = 0.08


def kinetic(values):
    padded = jnp.pad(values, ((2, 2), (2, 2), (2, 2), (0, 0)))
    centre = padded[2:-2, 2:-2, 2:-2]
    far_sum = (padded[4:, 2:-2, 2:-2] + padded[:-4, 2:-2, 2:-2]
               + padded[2:-2, 4:, 2:-2] + padded[2:-2, :-4, 2:-2]
               + padded[2:-2, 2:-2, 4:] + padded[2:-2, 2:-2, :-4])
    near_sum = (padded[3:-1, 2:-2, 2:-2] + padded[1:-3, 2:-2, 2:-2]
                + padded[2:-2, 3:-1, 2:-2] + padded[2:-2, 1:-3, 2:-2]
                + padded[2:-2, 2:-2, 3:-1] + padded[2:-2, 2:-2, 1:-3])
    laplace = (16.0 * near_sum - far_sum - 90.0 * centre) / 12.0
    return -0.5 * laplace


def relax_sweep(wave_set, local_potential):
    values = wave_set.astype(jnp.float32)
    update = kinetic(values) + local_potential[:, :, :, None] * values
    return (values - step_size * update).astype(jnp.bfloat16)


def wrap_fold(running, axis_dim, extent):
    inside = lax.slice_in_dim(running, B, B + extent, axis=axis_dim)
    below_rim = lax.slice_in_dim(running, 0, B, axis=axis_dim)
    above_rim = lax.slice_in_dim(running, B + extent, 2 * B + extent, axis=axis_dim)
    below_pad = [(0, 0), (0, 0), (0, 0)]
    above_pad = [(0, 0), (0, 0), (0, 0)]
    below_pad[axis_dim] = (extent - B, 0)
    above_pad[axis_dim] = (0, extent - B)
    return inside + jnp.pad(below_rim, below_pad) + jnp.pad(above_rim, above_pad)


def reference(wave_bands, potential, occupation, support, z_cuts, atom_state, atom_cell):
    domains = N_GX * N_GY * N_GZ
    band_count = wave_bands.shape[3]
    blocks = wave_bands.reshape(N_GX, DX, N_GY, DY, N_GZ, DZ, band_count).transpose(0, 2, 4, 1, 3, 5, 6).reshape(domains, DX, DY, DZ, band_count)
    weights = support.reshape(N_GX, DX, N_GY, DY, N_GZ, DZ).transpose(0, 2, 4, 1, 3, 5).reshape(domains, DX, DY, DZ)
    occupied = occupation.reshape(domains, band_count)
    wrapped = jnp.pad(potential, B, mode="wrap")
    domain_ids = jnp.arange(domains, dtype=jnp.int32)

    def one_domain(domain_item):
        wave_set, weight, band_weights, domain_id = domain_item
        index_x = domain_id // (N_GY * N_GZ)
        index_y = (domain_id // N_GZ) % N_GY
        index_z = domain_id % N_GZ
        local_potential = lax.dynamic_slice(wrapped, (index_x * CX, index_y * CY, index_z * CZ), (DX, DY, DZ))
        for sweep_index in range(SWEEPS):
            wave_set = relax_sweep(wave_set, local_potential)
        values = wave_set.astype(jnp.float32)
        return wave_set, weight * jnp.sum(values * values * band_weights, axis=-1)

    swept_sets, contributions = lax.map(one_domain, (blocks, weights, occupied, domain_ids))

    def deposit(domain_id, running):
        domain_id = domain_id.astype(jnp.int32)
        index_x = domain_id // (N_GY * N_GZ)
        index_y = (domain_id // N_GZ) % N_GY
        index_z = domain_id % N_GZ
        corner = (index_x * CX, index_y * CY, index_z * CZ)
        placed = lax.dynamic_slice(running, corner, (DX, DY, DZ))
        return lax.dynamic_update_slice(running, placed + contributions[domain_id], corner)

    padded_total = jnp.zeros((NX + 2 * B, NY + 2 * B, NZ + 2 * B), jnp.float32)
    padded_total = lax.fori_loop(0, domains, deposit, padded_total)
    density = wrap_fold(wrap_fold(wrap_fold(padded_total, 0, NX), 1, NY), 2, NZ)

    def recut(domain_id):
        index_z = domain_id % N_GZ
        follower = jnp.where(index_z < N_GZ - 1, domain_id + 1, domain_id)
        own_rows = swept_sets[domain_id]
        next_rows = lax.slice_in_dim(swept_sets[follower], 2 * B, 2 * B + DRIFT, axis=2)
        padding = jnp.zeros((DX, DY, DRIFT, band_count), jnp.bfloat16)
        joined = jnp.concatenate([own_rows, next_rows, padding], axis=2)
        start_row = (z_cuts[index_z] - index_z * CZ).astype(jnp.int32)
        window = lax.dynamic_slice_in_dim(joined, start_row, DZCAP, axis=2)
        extent = z_cuts[index_z + 1] - z_cuts[index_z] + 2 * B
        keep_rows = jnp.arange(DZCAP, dtype=jnp.int32) < extent
        return jnp.where(keep_rows[None, None, :, None], window, jnp.zeros((), jnp.bfloat16))

    recut_sets = lax.map(recut, domain_ids)
    new_bands = recut_sets.reshape(N_GX, N_GY, N_GZ, DX, DY, DZCAP, band_count).transpose(0, 3, 1, 4, 2, 5, 6).reshape(N_GX * DX, N_GY * DY, N_GZ * DZCAP, band_count)

    device_count = DEVICES
    cell_sets = atom_cell.reshape(device_count, ATOMS_DEV)
    state_sets = atom_state.reshape(COMP, device_count, ATOMS_DEV).transpose(1, 0, 2)
    slab_ids = jnp.arange(device_count, dtype=jnp.int32) % N_GZ
    follow_cells = jnp.roll(cell_sets, -1, axis=0)
    follow_states = jnp.roll(state_sets, -1, axis=0)

    def settle(own_state, own_cells, slab_index, next_state, next_cells):
        staying = own_cells >= z_cuts[slab_index]
        arriving = jnp.logical_and(slab_index < N_GZ - 1, next_cells < z_cuts[slab_index + 1])
        stay_slot = jnp.where(staying, jnp.cumsum(staying.astype(jnp.int32)) - 1, ACAP)
        stay_total = jnp.sum(staying.astype(jnp.int32))
        arrive_slot = jnp.where(arriving, stay_total + jnp.cumsum(arriving.astype(jnp.int32)) - 1, ACAP)
        placed_state = jnp.zeros((COMP, ACAP), jnp.float32)
        placed_state = placed_state.at[:, stay_slot].set(own_state, mode="drop")
        placed_state = placed_state.at[:, arrive_slot].set(next_state, mode="drop")
        placed_cells = jnp.full((ACAP,), -1, jnp.int32)
        placed_cells = placed_cells.at[stay_slot].set(own_cells, mode="drop")
        placed_cells = placed_cells.at[arrive_slot].set(next_cells, mode="drop")
        return placed_state, placed_cells

    settled_states, settled_cells = jax.vmap(settle)(state_sets, cell_sets, slab_ids, follow_states, follow_cells)
    new_atoms = settled_states.transpose(1, 0, 2).reshape(COMP, device_count * ACAP)
    new_cells = settled_cells.reshape(device_count * ACAP)
    return (density, new_bands, new_atoms, new_cells)
```

```python
import functools
import numpy as np
import jax
import jax.numpy as jnp
from jax import lax
from jax.experimental import pallas as pl
from jax.experimental.pallas import tpu as pltpu
from jax.sharding import PartitionSpec as P
import ml_dtypes

B = 8
COMP = 4
CX = 8
CZ = 16
DX = 24
DZ = 32
DRIFT = 8
DZCAP = 40
ACAP = 256
NB = 256
N_GX = 4
N_GY = 4
N_GZ = 8
YB = 8
YR = 6
ROWS = YB * DZ
PLANE = DX * DZ
RING = 8
VMEM_BYTES = 48 * 1024 * 1024

CENTRE = 210.0 / 16.0
FAR = 1.0 / 16.0
POT = -24.0 / 16.0
SCALE = 16.0 / 300.0

CHUNKS = (((0, 4),), ((4, 8), (8, 12)), ((12, 16), (16, 20), (20, 24)))


def stencil_matrix():
    out = np.zeros((YB + 4, DZ, YB, DZ), np.float32)
    for y in range(YB + 4):
        for k in range(YB):
            gap = abs(y - 2 - k)
            for z in range(DZ):
                if gap == 0:
                    out[y, z, k, z] = CENTRE
                    for step, value in ((1, 1.0), (2, -FAR)):
                        for side in (z - step, z + step):
                            if 0 <= side < DZ:
                                out[y, z, k, side] = value
                elif gap == 1:
                    out[y, z, k, z] = 1.0
                elif gap == 2:
                    out[y, z, k, z] = -FAR
    return out.reshape((YB + 4) * DZ, ROWS).astype(ml_dtypes.bfloat16)


def sweep_pieces(ring, matrix_ref, x):
    here = ring[x & 7]
    cells = jnp.concatenate([here[ROWS * block : ROWS * block + ROWS] for block in range(3)], axis=1)
    product = jnp.dot(matrix_ref[...], cells, preferred_element_type=jnp.float32)

    def part(block, row):
        return product[row : row + 64, NB * block : NB * block + NB]

    for piece in range(12):
        block, inner = divmod(piece, 4)
        total = part(block, 64 + 64 * inner)
        if inner == 3 and block < 2:
            total = total + part(block + 1, 0)
        if inner == 0 and block > 0:
            total = total + part(block - 1, 320)
        rows = slice(64 * piece, 64 * piece + 64)
        near = ring[(x - 1) & 7, rows] + ring[(x + 1) & 7, rows]
        far = ring[(x - 2) & 7, rows] + ring[(x + 2) & 7, rows]
        yield piece, rows, total, near - far * jnp.bfloat16(FAR)


def clear_outside(ring, first, plane):
    if first == 0:

        @pl.when(pl.program_id(0) == 0)
        def _():
            ring[RING - 2] = jnp.zeros_like(ring[0])
            ring[RING - 1] = jnp.zeros_like(ring[0])

    @pl.when(plane >= DX)
    def _():
        ring[plane & 7] = jnp.zeros_like(ring[0])


def stencil_kernel(x0, x1, first, v_ref, matrix_ref, *rest):
    out_ref, ring = rest[-2:]
    plane = first + pl.program_id(0)
    clear_outside(ring, first, plane)

    @pl.when(plane < DX)
    def _():
        ring[plane & 7] = v_ref[0]

    x = plane - 2

    @pl.when(x >= x0)
    def _():
        for _, rows, total, rest_of_it in sweep_pieces(ring, matrix_ref, x):
            out_ref[0, rows] = (total + rest_of_it.astype(jnp.float32)).astype(jnp.bfloat16)


def whole(shape):
    return pl.BlockSpec(shape, lambda i: (0,) * len(shape))


def settings(moved=0):
    return dict(
        compiler_params=pltpu.CompilerParams(
            vmem_limit_bytes=VMEM_BYTES, dimension_semantics=("arbitrary",)
        ),
        cost_estimate=pl.CostEstimate(flops=0, bytes_accessed=moved, transcendentals=0),
    )


def stencil_chunk(x0, x1, bands, matrix, so_far):
    first = max(0, x0 - 2)
    in_specs = [
        pl.BlockSpec((1, PLANE, NB), lambda i: (jnp.minimum(first + i, DX - 1), 0, 0)),
        whole((384, ROWS)),
    ]
    args = [bands, matrix]
    aliases = {}
    if so_far is not None:
        in_specs.append(pl.BlockSpec(memory_space=pl.ANY))
        args.append(so_far)
        aliases = {2: 0}
    return pl.pallas_call(
        functools.partial(stencil_kernel, x0, x1, first),
        grid=(x1 + 2 - first,),
        in_specs=in_specs,
        out_specs=pl.BlockSpec((1, PLANE, NB), lambda i: (jnp.maximum(first + i - 2, x0), 0, 0)),
        out_shape=jax.ShapeDtypeStruct((DX, PLANE, NB), jnp.bfloat16),
        scratch_shapes=[pltpu.VMEM((RING, PLANE, NB), jnp.bfloat16)],
        input_output_aliases=aliases,
        name=f"stencil_{x0}",
        **settings(),
    )(*args)


def sweep_kernel(
    x0, x1, first, parts,
    v_ref, once_ref, below_ref, own_ref, above_ref, occ_ref, support_ref, matrix_ref,
    *rest,
):
    swept_ref, dens_ref = rest[:2]
    send_refs = rest[2 : 2 + len(parts)]
    ring, pot_ring, pot_cells, turn, leaving = rest[2 + len(parts) :]
    step = pl.program_id(0)
    plane = first + step
    clear_outside(ring, first, plane)

    @pl.when(step == 0)
    def _():
        turn[...] = jnp.zeros_like(turn)
        for ref, low, high, at in ((below_ref, 8, 16, 0), (own_ref, 0, 16, 8), (above_ref, 0, 8, 24)):
            turn[0:72] = ref[0:72] * POT
            turned = turn[...].T
            for y in range(YB):
                pot_cells[DZ * y + at : DZ * y + at + high - low] = turned[CZ * y + low : CZ * y + high]

    @pl.when(plane < DX)
    def _():
        cells = pot_cells[...].astype(jnp.bfloat16)
        lines = lax.broadcasted_iota(jnp.int32, (128, 3 * 128), 0)
        blocks = lax.broadcasted_iota(jnp.int32, (128, 3 * 128), 1) >> 7
        chosen = jnp.where(lines == blocks * DX + plane, 1.0, 0.0).astype(jnp.bfloat16)
        spread = jnp.dot(cells, chosen, preferred_element_type=jnp.float32).astype(jnp.bfloat16)
        for block in range(3):
            rows = slice(ROWS * block, ROWS * block + ROWS)
            pot = spread[:, 128 * block : 128 * block + 128]
            pot_ring[plane & 7, rows] = pot
            ring[plane & 7, rows] = once_ref[0, rows] + jnp.concatenate([pot, pot], axis=1) * v_ref[0, rows]

    x = plane - 2

    @pl.when(x >= x0)
    def _():
        for piece, rows, total, rest_of_it in sweep_pieces(ring, matrix_ref, x):
            pot = pot_ring[x & 7, rows]
            rest_of_it = rest_of_it + jnp.concatenate([pot, pot], axis=1) * ring[x & 7, rows]
            total = (total + rest_of_it.astype(jnp.float32)) * (SCALE * SCALE)
            swept_ref[0, rows] = total.astype(jnp.bfloat16)
            down = total.reshape(2, DZ, NB)[:, 2 * B : 2 * B + DRIFT].reshape(2 * DRIFT, NB)
            leaving[16 * piece : 16 * piece + 16] = down.astype(jnp.bfloat16)
        for send_ref, (low, high) in zip(send_refs, parts):

            @pl.when(jnp.logical_and(x >= low, x < high))
            def _(send_ref=send_ref):
                send_ref[0] = leaving[...]

        occ = occ_ref[...]
        coarse = occ.astype(jnp.bfloat16).astype(jnp.float32)
        line = lax.broadcasted_iota(jnp.int32, (16, NB), 0)
        weights = jnp.where(line == 0, coarse, jnp.where(line == 1, occ - coarse, 0.0)).astype(jnp.bfloat16)
        cells = swept_ref[0]
        sums = lax.dot_general(
            weights, cells * cells, (((1,), (1,)), ((), ())), preferred_element_type=jnp.float32
        )
        dens_ref[pl.ds(x - x0, 1), :] = (sums[0:1] + sums[1:2]) * support_ref[pl.ds(x, 1), :]


def sweep_chunk(parts, bands, once, pots, occ, support, matrix):
    x0, x1 = parts[0][0], parts[-1][1]
    first = max(0, x0 - 2)
    in_plane = lambda i: (jnp.minimum(first + i, DX - 1), 0, 0)
    out_plane = lambda low, high: (lambda i: (jnp.clip(first + i - 2, low, high - 1) - low, 0, 0))
    planes = x1 - x0
    out = pl.pallas_call(
        functools.partial(sweep_kernel, x0, x1, first, parts),
        grid=(x1 + 2 - first,),
        in_specs=[
            pl.BlockSpec((1, PLANE, NB), in_plane),
            pl.BlockSpec((1, PLANE, NB), in_plane),
            whole((72, 128)),
            whole((72, 128)),
            whole((80, 128)),
            whole((1, NB)),
            whole((DX, PLANE)),
            whole((384, ROWS)),
        ],
        out_specs=[
            pl.BlockSpec((1, PLANE, NB), out_plane(x0, x1)),
            whole((planes, PLANE)),
        ]
        + [pl.BlockSpec((1, DX * DRIFT, NB), out_plane(low, high)) for low, high in parts],
        out_shape=[
            jax.ShapeDtypeStruct((planes, PLANE, NB), jnp.bfloat16),
            jax.ShapeDtypeStruct((planes, PLANE), jnp.float32),
        ]
        + [jax.ShapeDtypeStruct((high - low, DX * DRIFT, NB), jnp.bfloat16) for low, high in parts],
        scratch_shapes=[
            pltpu.VMEM((RING, PLANE, NB), jnp.bfloat16),
            pltpu.VMEM((RING, PLANE, 128), jnp.bfloat16),
            pltpu.VMEM((ROWS, 128), jnp.float32),
            pltpu.VMEM((128, 128), jnp.float32),
            pltpu.VMEM((DX * DRIFT, NB), jnp.bfloat16),
        ],
        name=f"sweeps_{x0}",
        **settings(planes * 10 * PLANE * NB if x0 else 0),
    )(bands, once, *pots, occ, support, matrix)
    return out[0], out[1], out[2:]


def recut_tables():
    line_y, line = np.divmod(np.arange(YR * DZCAP), DZCAP)
    own_y, own_z = np.divmod(np.arange(YR * DZ), DZ)
    next_y, next_z = np.divmod(np.arange(YR * DRIFT), DRIFT)
    y = np.concatenate([own_y, next_y])
    z = np.concatenate([own_z, next_z + DZ])
    shift = np.where(line_y[:, None] == y[None, :], z[None, :] - line[:, None], -1000)
    return shift.astype(np.int32), np.broadcast_to(z[None, :], (8, z.size)).astype(np.int32)


def recut_kernel(cuts_ref, shift_ref, source_ref, swept_ref, next_ref, *rest):
    out_ref, matrix = rest[-2:]

    @pl.when(pl.program_id(0) == 0)
    def _():
        c = lax.axis_index("gz")
        start_row = cuts_ref[c] - c * CZ
        last_row = cuts_ref[c + 1] - c * CZ + 2 * B
        chosen = jnp.logical_and(shift_ref[...] == start_row, source_ref[0:1] < last_row)
        matrix[...] = jnp.where(chosen, 1.0, 0.0).astype(jnp.bfloat16)

    columns = [
        jnp.concatenate(
            [swept_ref[0, YR * DZ * k : YR * DZ * (k + 1)], next_ref[0, YR * DRIFT * k : YR * DRIFT * (k + 1)]],
            axis=0,
        )
        for k in range(DX // YR)
    ]
    window = jnp.dot(matrix[...], jnp.concatenate(columns, axis=1), preferred_element_type=jnp.float32)
    for k in range(DX // YR):
        rows = window[:, NB * k : NB * k + NB].reshape(YR, DZCAP, NB)
        out_ref[0, YR * k : YR * k + YR] = rows.astype(jnp.bfloat16)


def recut(swept, x0, low, high, next_rows, z_cuts, so_far):
    shift, source = recut_tables()
    in_specs = [
        pl.BlockSpec(memory_space=pltpu.SMEM),
        whole(shift.shape),
        whole(source.shape),
        pl.BlockSpec((1, PLANE, NB), lambda i: (i + low - x0, 0, 0)),
        pl.BlockSpec((1, DX * DRIFT, NB), lambda i: (i, 0, 0)),
    ]
    args = [z_cuts, jnp.asarray(shift), jnp.asarray(source), swept, next_rows]
    aliases = {}
    if so_far is not None:
        in_specs.append(pl.BlockSpec(memory_space=pl.ANY))
        args.append(so_far)
        aliases = {5: 0}
    return pl.pallas_call(
        recut_kernel,
        grid=(high - low,),
        in_specs=in_specs,
        out_specs=pl.BlockSpec((1, DX, DZCAP, NB), lambda i: (i + low, 0, 0, 0)),
        out_shape=jax.ShapeDtypeStruct((DX, DX, DZCAP, NB), jnp.bfloat16),
        scratch_shapes=[pltpu.VMEM(shift.shape, jnp.bfloat16)],
        input_output_aliases=aliases,
        name=f"recut_{low}",
        **settings(),
    )(*args)


def both_sides(low, high, axis):
    size = lax.axis_size(axis)
    up = [(i, (i + 1) % size) for i in range(size)]
    down = [(j, i) for i, j in up]
    return lax.ppermute(low, axis, down), lax.ppermute(high, axis, up)


def from_behind(shard, axis, by):
    size = lax.axis_size(axis)
    pairs = [(i, i + by) for i in range(size) if 0 <= i + by < size]
    return lax.ppermute(shard, axis, pairs)


def atoms_kernel(cuts_ref, own_ref, arrivals_ref, atoms_ref, cells_ref):
    c = lax.axis_index("gz")
    slots = own_ref.shape[1]
    state = jnp.concatenate([own_ref[...], arrivals_ref[...]], axis=1)
    cells = state[COMP : COMP + 1] - 1.0
    lane = lax.broadcasted_iota(jnp.int32, (1, 2 * slots), 1)
    here = cells >= cuts_ref[c].astype(jnp.float32)
    comes = jnp.logical_and(cells < cuts_ref[c + 1].astype(jnp.float32), c + 1 < lax.axis_size("gz"))
    taken = jnp.where(lane < slots, jnp.where(here, 1.0, 0.0), jnp.where(comes, 1.0, 0.0))
    column = jnp.broadcast_to(taken, (128, 2 * slots)).T
    source = lax.broadcasted_iota(jnp.int32, (2 * slots, 2 * slots), 0)
    target = lax.broadcasted_iota(jnp.int32, (2 * slots, 2 * slots), 1)
    before = jnp.where(target <= source, 1.0, 0.0).astype(jnp.bfloat16)
    count = jnp.dot(before, column.astype(jnp.bfloat16), preferred_element_type=jnp.float32)
    count = jnp.concatenate([count, count], axis=1)
    column = jnp.concatenate([column, column], axis=1)
    chosen = jnp.logical_and(column > 0.5, count - 1.0 == target.astype(jnp.float32))
    table = jnp.where(chosen, 1.0, 0.0).astype(jnp.bfloat16)
    high = state.astype(jnp.bfloat16).astype(jnp.float32)
    middle = (state - high).astype(jnp.bfloat16).astype(jnp.float32)
    parts = jnp.concatenate([high, middle, state - high - middle, jnp.zeros_like(high)], axis=0)
    placed = jnp.dot(parts.astype(jnp.bfloat16), table, preferred_element_type=jnp.float32)
    placed = placed[0:8] + placed[8:16] + placed[16:24]
    atoms_ref[...] = placed[0:COMP]
    cells_ref[...] = placed[COMP : COMP + 1].astype(jnp.int32) - 1


def place_atoms(z_cuts, own, arrivals):
    vmem = pl.BlockSpec(memory_space=pltpu.VMEM)
    atoms, cells = pl.pallas_call(
        atoms_kernel,
        in_specs=[pl.BlockSpec(memory_space=pltpu.SMEM), vmem, vmem],
        out_specs=[vmem, vmem],
        out_shape=[
            jax.ShapeDtypeStruct((COMP, ACAP), jnp.float32),
            jax.ShapeDtypeStruct((1, ACAP), jnp.int32),
        ],
        name="atoms",
    )(z_cuts, own, arrivals)
    return atoms, cells.reshape(ACAP)


def local(wave_bands, potential, occupation, support, z_cuts, atom_state, atom_cell):
    bands = wave_bands.reshape(DX, PLANE, NB)
    occ = occupation.reshape(1, NB)
    weights = support.reshape(DX, PLANE)
    matrix = jnp.asarray(stencil_matrix())

    pots = potential.reshape(CX, YB * CZ)
    once = None
    for axis, (x0, x1) in zip(("gx", "gy"), ((0, 8), (8, 16))):
        after, before = both_sides(pots, pots, axis)
        once = stencil_chunk(x0, x1, bands, matrix, once)
        pots = jnp.concatenate([before, pots, after], axis=0)
        pots, once = lax.optimization_barrier((pots, once))
    atoms = jnp.concatenate(
        [atom_state, (atom_cell + 1).astype(jnp.float32)[None, :], jnp.zeros((3, atom_cell.size), jnp.float32)],
        axis=0,
    )
    after, before = both_sides(jnp.concatenate([pots, atoms], axis=0), pots, "gz")
    once = stencil_chunk(16, 24, bands, matrix, once)
    arriving_atoms = after[72:]
    pots = (before, pots, after)

    swept, dens, arrivals = [], [], []
    new_bands = None
    for index, parts in enumerate(CHUNKS):
        if index == 2:
            new_bands = recut(swept[0], 0, *CHUNKS[0][0], arrivals[0][0], z_cuts, None)
            occ, new_bands = lax.optimization_barrier((occ, new_bands))
        chunk, chunk_dens, sends = sweep_chunk(parts, bands, once, pots, occ, weights, matrix)
        swept.append(chunk)
        occ, chunk_dens = lax.optimization_barrier((occ, chunk_dens))
        dens.append(chunk_dens)
        arrivals.append([from_behind(send, "gz", -1) for send in sends])

    pieces = [
        (index, parts[0][0], low, high, arrival)
        for index, parts in enumerate(CHUNKS)
        for arrival, (low, high) in zip(arrivals[index], parts)
    ][1:]

    def recut_next(new_bands):
        index, x0, low, high, arrival = pieces.pop(0)
        return recut(swept[index], x0, low, high, arrival, z_cuts, new_bands)

    low_side = jnp.concatenate([dens[0], dens[1][:4]], axis=0)
    from_above, from_below = both_sides(low_side, dens[2][4:], "gx")
    inside = jnp.concatenate([dens[1][4:], dens[2][:4]], axis=0)
    new_bands = recut_next(recut_next(new_bands))
    from_above, from_below, new_bands = lax.optimization_barrier((from_above, from_below, new_bands))
    dens = inside + from_above + from_below
    from_above, from_below = both_sides(dens[:, :ROWS], dens[:, 2 * ROWS :], "gy")
    dens = dens[:, ROWS : 2 * ROWS] + from_above + from_below
    while len(pieces) > 1:
        new_bands = recut_next(new_bands)
    dens, new_bands = lax.optimization_barrier((dens, new_bands))
    from_above, from_below = both_sides(dens, dens, "gz")
    shape = (CX, YB, DZ)
    inside = dens.reshape(shape)[:, :, B : B + CZ]
    lower = from_below.reshape(shape)[:, :, B + CZ :]
    upper = from_above.reshape(shape)[:, :, :B]
    density = inside + jnp.concatenate([lower, upper], axis=2)
    new_bands = recut_next(new_bands)

    new_atoms, new_cells = place_atoms(z_cuts, atoms, arriving_atoms)
    return (density, new_bands, new_atoms, new_cells)


def solution(mesh):
    in_specs = (
        P("gx", "gy", "gz", None),
        P("gx", "gy", "gz"),
        P("gx", "gy", "gz", None),
        P("gx", "gy", "gz"),
        P(),
        P(None, ("gx", "gy", "gz")),
        P(("gx", "gy", "gz")),
    )
    out_specs = (
        P("gx", "gy", "gz"),
        P("gx", "gy", "gz", None),
        P(None, ("gx", "gy", "gz")),
        P(("gx", "gy", "gz")),
    )
    return jax.shard_map(local, mesh=mesh, in_specs=in_specs, out_specs=out_specs, check_vma=False)
```
